32 devices in a mesh: grp: 2 (over y), gx: 8 (over z, x), gy: 2 (over core).
Axes of the slice: x: 2, y: 2, z: 4, core: 2. Of those that a mesh axis runs over, the one named last changes fastest.
Arguments:
- images: bfloat16 [8, 1024, 2048], P('grp', 'gx', 'gy'), parts along dimension 0, may hold values from 0.049804688 to 5
- weights: bfloat16 [4, 4, 3, 64, 1024], P(None, None, None, None, 'gx'), may hold values from 3.886223e-05 to 0.0390625
- crossings: int32 [4, 4, 8, 3], P(None, None, 'gx'), may hold values from 0 to 3, as said below
- counts: int32 [4, 4, 8], P(None, None, 'gx'), may hold values from 2 to 3, as said below
Outputs:
- smoothed: float32 [8, 1024, 2048], P('grp', 'gx', 'gy'), parts along dimension 0
The draws below stay inside these ranges and needn't reach their ends.
There are 2 independent parts, one for each index of `grp`. The reference program is written for one: setup_inputs(seed, part) draws one part's arguments, and reference() takes and returns one part's arrays. A program takes and returns all parts, laid end to end along the dimension named above; an argument that names none is the same for every part. Nothing has to cross between parts.
Inputs may be any that keep to these rules, and one draw needn't show every extreme that they name: `crossings`: each list names 3 different window blocks in rising order. Only the first counts[c, z, i] entries of a list are crossed; the remaining entries are not used.
All inputs are finite; a program needn't handle non-finite values.
Results may differ from the reference program's by a relative error of at most 0.0003.
Values may be sent and summed in bfloat16 or wider, within the bound.
A program may use at most 64 MiB of HBM per device.

```python
import math
import jax
import jax.numpy as jnp
from jax import lax

CAMS = 4
DEPTH = 4
TILE = 128
SUB = 64
KMAX = 3
PASSES = 3
WIN = 4
X = 1024
Y = 2048
N_GX = 8


def draw_crossings(key, part):
    key = jax.random.fold_in(key, 11)
    total = CAMS * DEPTH * N_GX
    omitted = jax.random.randint(key, (total,), 0, WIN)
    omitted = omitted.at[0].set(0).at[1].set(WIN - 1)
    ladder = jnp.arange(KMAX, dtype=jnp.int32)
    lists = ladder[None, :] + (ladder[None, :] >= omitted[:, None]).astype(jnp.int32)
    return lists.reshape(CAMS, DEPTH, N_GX, KMAX).astype(jnp.int32)


def draw_counts(key, part):
    key = jax.random.fold_in(key, 23)
    total = CAMS * DEPTH * N_GX
    values = jax.random.randint(key, (total,), 2, KMAX + 1)
    values = values.at[0].set(KMAX).at[1].set(2)
    return values.reshape(CAMS, DEPTH, N_GX).astype(jnp.int32)


def steps_of(key, extent, pieces, smallest, top_value):
    gain, own = 1.0, jax.random.fold_in(key, 6)
    for dim, blocks in pieces:
        heights = jnp.exp(jax.random.uniform(jax.random.fold_in(own, dim), (blocks,), jnp.float32, smallest / len(pieces), top_value / len(pieces)))
        gain = gain * jnp.repeat(heights, extent[dim] // blocks).reshape([-1 if axis == dim else 1 for axis in range(len(extent))])
    return gain


def setup_inputs(seed: int = 0, part: int = 0) -> dict:
    key_list = jax.random.split(jax.random.key(seed), 5)
    part_splits = jax.random.split(jax.random.fold_in(key_list[4], part), 5)
    images = jnp.clip(jnp.exp(math.log(5.0) - 4.609084 * jax.random.uniform(part_splits[0], (CAMS, X, Y), jnp.float32) ** steps_of(part_splits[0], (CAMS, X, Y), ((1, 8), (2, 2)), -0.2, 0.2)), 0.049804688, 5.0).astype(jnp.bfloat16)
    weights = jnp.clip(jnp.exp(math.log(0.0390625) - 6.912895 * jax.random.uniform(key_list[1], (CAMS, DEPTH, KMAX, SUB, X), jnp.float32) ** steps_of(key_list[1], (CAMS, DEPTH, KMAX, SUB, X), ((4, 8),), -0.2, 0.2)), 3.886222839355469e-05, 0.0390625).astype(jnp.bfloat16)
    crossings = draw_crossings(jax.random.fold_in(key_list[4], 71), part)
    counts = draw_counts(jax.random.fold_in(key_list[4], 71), part)
    return {"images": images, "weights": weights, "crossings": crossings, "counts": counts}


def binomial(field):
    padded = jnp.pad(field, 1)
    along_z = 0.25 * padded[:-2] + 0.5 * padded[1:-1] + 0.25 * padded[2:]
    along_x = 0.25 * along_z[:, :-2] + 0.5 * along_z[:, 1:-1] + 0.25 * along_z[:, 2:]
    return 0.25 * along_x[:, :, :-2] + 0.5 * along_x[:, :, 1:-1] + 0.25 * along_x[:, :, 2:]


def reference(images, weights, crossings, counts):
    padded = jnp.pad(images, ((0, 0), (SUB, SUB), (0, 0)))
    slot_ids = jnp.arange(KMAX, dtype=jnp.int32)
    block_ids = jnp.arange(WIN, dtype=jnp.int32)

    def one_slab(slab_index):
        offset = (slab_index * TILE).astype(jnp.int32)
        window = lax.dynamic_slice_in_dim(padded, offset, WIN * SUB, 1).astype(jnp.float32)
        active = slot_ids[None, None, :] < counts[:, :, slab_index][:, :, None]
        crossed = crossings[:, :, slab_index, :]
        chosen_ids = ((crossed[:, :, :, None] == block_ids[None, None, None, :]) & active[:, :, :, None]).astype(jnp.float32)
        slab_weights = lax.dynamic_slice_in_dim(weights, offset, TILE, 4).astype(jnp.float32)
        spread = jnp.einsum("czkw,czksx->czwsx", chosen_ids, slab_weights, precision=lax.Precision.HIGHEST)
        spread = spread.reshape(CAMS, DEPTH, WIN * SUB, TILE)
        projection = jnp.einsum("czrx,cry->czxy", spread, window, precision=lax.Precision.HIGHEST)
        product = projection[0]
        for camera in range(1, CAMS):
            product = product * projection[camera]
        return product

    stacked = lax.map(one_slab, jnp.arange(N_GX, dtype=jnp.int32))
    product = jnp.transpose(stacked, (1, 0, 2, 3)).reshape(DEPTH, X, Y)
    smoothed = product
    for pass_index in range(PASSES):
        smoothed = binomial(smoothed)
    return smoothed
```

```python
import functools

import jax
import jax.numpy as jnp
import numpy as np
from jax import lax
from jax.experimental import pallas as pl
from jax.experimental.pallas import tpu as pltpu
from jax.sharding import PartitionSpec as P

PASSES = 3
CHUNKS = 4
LANES = 128
BF = jnp.bfloat16
F32 = jnp.float32


def taps(distance):
    distance = jnp.abs(distance)
    value = jnp.where(distance == 0, 20.0, 0.0)
    for far, weight in ((1, 15.0), (2, 6.0), (3, 1.0)):
        value = jnp.where(distance == far, weight, value)
    return value.astype(F32)


def iota(shape, dim):
    return lax.broadcasted_iota(jnp.int32, shape, dim)


def layer_matrix(depth):
    step = 0.5 * np.eye(depth) + 0.25 * (np.eye(depth, k=1) + np.eye(depth, k=-1))
    return np.linalg.matrix_power(step, PASSES)


def split(value):
    high = value.astype(BF)
    return high, (value - high.astype(F32)).astype(BF)


def dot(a, b):
    return jnp.dot(a, b, preferred_element_type=F32)


def kernel(dims, lists, counts, images, weights, out,
           window, stack, spread, prod, part, field, done, out_stage, across, along, edge, pick, beside,
           outbox, inbox, img_send, img_recv, halo_send, halo_recv, seam_sem, local_sem, out_sem):
    cams, depth, slots, sub, tile, cols, n_gx = dims
    width = cols // CHUNKS
    blocks = tile // sub + 2
    gx, gy = lax.axis_index("gx"), lax.axis_index("gy")
    has_lo, has_hi = gx > 0, gx < n_gx - 1
    first = jnp.where(has_lo, 0.0, 1.0).astype(F32)
    last = jnp.where(has_hi, 0.0, 1.0).astype(F32)
    lo, hi, peer = {"gx": gx - 1}, {"gx": gx + 1}, {"gy": 1 - gy}

    def offset(j):
        return pl.multiple_of(jnp.where(gy == 0, (CHUNKS - 1 - j) * width, j * width), width)

    barrier = pltpu.get_barrier_semaphore()

    @pl.when(has_lo)
    def _():
        pl.semaphore_signal(barrier, inc=1, device_id=lo, device_id_type=pl.DeviceIdType.MESH)

    @pl.when(has_hi)
    def _():
        pl.semaphore_signal(barrier, inc=1, device_id=hi, device_id_type=pl.DeviceIdType.MESH)

    pl.semaphore_signal(barrier, inc=1, device_id=peer, device_id_type=pl.DeviceIdType.MESH)

    load_w = pltpu.make_async_copy(weights, stack, local_sem.at[0])
    load_i = pltpu.make_async_copy(images, window.at[:, pl.ds(sub, tile), :], local_sem.at[1])
    load_w.start()
    load_i.start()

    pl.semaphore_wait(barrier, 1 + jnp.where(has_lo, 1, 0) + jnp.where(has_hi, 1, 0))

    def remote(src, dst, send, recv, where):
        return pltpu.make_async_remote_copy(
            src_ref=src, dst_ref=dst, send_sem=send, recv_sem=recv,
            device_id=where, device_id_type=pl.DeviceIdType.MESH)

    def image_copy(j, up):
        cut = pl.ds(offset(j), width)
        if up:
            return remote(images.at[:, pl.ds(tile - sub, sub), cut], window.at[:, pl.ds(0, sub), cut],
                          img_send.at[0, j], img_recv.at[0, j], hi)
        return remote(images.at[:, pl.ds(0, sub), cut], window.at[:, pl.ds(tile + sub, sub), cut],
                      img_send.at[1, j], img_recv.at[1, j], lo)

    def halo_copy(j, up):
        if up:
            return remote(outbox.at[j, pl.ds(16, 16)], inbox.at[j, pl.ds(0, 16)],
                          halo_send.at[0, j], halo_recv.at[0, j], hi)
        return remote(outbox.at[j, pl.ds(0, 16)], inbox.at[j, pl.ds(16, 16)],
                      halo_send.at[1, j], halo_recv.at[1, j], lo)

    def both(make, send, recv):
        def act(copy, start, finish):
            if start:
                copy.start()
            if finish == "send":
                copy.wait_send()
            if finish == "recv":
                copy.wait_recv()

        if send is not None:
            pl.when(has_hi)(lambda: act(make(True), send == "start", send))
            pl.when(has_lo)(lambda: act(make(False), send == "start", send))
        if recv is not None:
            pl.when(has_lo)(lambda: act(make(True), False, "recv"))
            pl.when(has_hi)(lambda: act(make(False), False, "recv"))

    for j in range(CHUNKS):
        both(functools.partial(image_copy, j), "start", None)

    @pl.when(jnp.logical_not(has_lo))
    def _():
        window[:, pl.ds(0, sub), :] = jnp.zeros((cams, sub, cols), BF)
        inbox[:, pl.ds(0, 16), :] = jnp.zeros((CHUNKS, 16, width), BF)

    @pl.when(jnp.logical_not(has_hi))
    def _():
        window[:, pl.ds(tile + sub, sub), :] = jnp.zeros((cams, sub, cols), BF)
        inbox[:, pl.ds(16, 16), :] = jnp.zeros((CHUNKS, 16, width), BF)

    outer = pl.multiple_of(jnp.where(gy == 0, 0, cols + LANES), LANES)
    inner = pl.multiple_of(jnp.where(gy == 0, cols + LANES, 0), LANES)
    field[:, :, pl.ds(outer, LANES)] = jnp.zeros((2, depth * tile, LANES), BF)

    i, k = iota((tile, tile), 0), iota((tile, tile), 1)
    along[...] = ((taps(i - k) - first * taps(i + k + 2) - last * taps(2 * tile - i - k)) / 64).astype(BF)
    r, k = iota((depth * tile, 32), 0), iota((depth * tile, 32), 1)
    q, zz = k % 4, (k // 4) % depth
    place = jnp.where(k < 16, q - 3, tile + q)
    near = jnp.where((q < 3) & (zz == r // tile), taps(r % tile - place), 0.0)
    beside[...] = (near / 64).astype(BF)
    k, r = iota((32, depth * tile), 0), iota((32, depth * tile), 1)
    q, zz = k % 4, (k // 4) % depth
    place = zz * tile + jnp.where(k < 16, q, tile - 3 + q)
    pick[...] = jnp.where((q < 3) & (place == r), 1.0, 0.0).astype(BF)
    a, b = iota((width + 2 * LANES, width), 0) - LANES, iota((width + 2 * LANES, width), 1)
    across[...] = (taps(a - b) / 64).astype(BF)
    mirror = jnp.where(gy == 0, a + b + 2, 2 * width - a - b)
    mirror = jnp.where((a >= 0) & (a < width), mirror, 4)
    edge[...] = ((taps(a - b) - taps(mirror)) / 64).astype(BF)

    load_w.wait()
    for c in range(cams):
        for z in range(depth):
            mats = [stack[c, z, s].astype(F32) for s in range(slots)]
            rows = []
            for w in range(blocks):
                total = None
                for s in range(slots):
                    used = (lists[c, s, 0, z] == w) & (s < counts[c, 0, z])
                    term = mats[s] * jnp.where(used, 1.0, 0.0).astype(F32)
                    total = term if total is None else total + term
                rows.append(total)
            whole = jnp.concatenate(rows, axis=0)
            spread[c, pl.ds(z * tile, tile), :] = jnp.transpose(whole).astype(BF)
    load_i.wait()

    layers = layer_matrix(depth)

    def project(j):
        cut = pl.ds(offset(j), width)
        both(functools.partial(image_copy, j), None, "recv")
        for c in range(cams):
            now = dot(spread[c], window[c, :, cut])
            if c == 0:
                prod[...] = now
            else:
                prod[...] = prod[...] * now
        for z in range(depth):
            total = None
            for s in range(depth):
                if layers[z, s] != 0.0:
                    term = prod[pl.ds(s * tile, tile), :] * float(layers[z, s])
                    total = term if total is None else total + term
            high, low = split(total)
            part[0, pl.ds(z * tile, tile), :] = high
            part[1, pl.ds(z * tile, tile), :] = low
        outbox[j] = dot(pick[...], part[0]).astype(BF)
        both(functools.partial(halo_copy, j), "start", None)
        for z in range(depth):
            rows = pl.ds(z * tile, tile)
            done[j % 2, rows, :] = dot(along[...], part[0, rows, :]) + dot(along[...], part[1, rows, :])

    def finish_x(j):
        both(functools.partial(halo_copy, j), None, "recv")
        high, low = split(done[j % 2] + dot(beside[...], inbox[j]))
        cut = pl.ds(pl.multiple_of(offset(j) + LANES, LANES), width)
        field[0, :, cut] = high
        field[1, :, cut] = low

    mine = pl.multiple_of(jnp.where(gy == 0, cols, LANES), LANES)
    theirs = pl.multiple_of(jnp.where(gy == 0, 0, cols + LANES), LANES)
    seam = remote(field.at[:, :, pl.ds(mine, LANES)], field.at[:, :, pl.ds(theirs, LANES)],
                  seam_sem.at[0], seam_sem.at[1], peer)

    def store(j):
        return pltpu.make_async_copy(
            out_stage.at[j], out.at[:, :, pl.ds(offset(j), width)], out_sem.at[j])

    def finish_y(j):
        if j == 0:
            seam.wait_recv()
        cut = pl.ds(offset(j), width + 2 * LANES)
        mat = (edge if j == CHUNKS - 1 else across)[...]
        full = dot(field[0, :, cut], mat) + dot(field[1, :, cut], mat)
        out_stage[j] = full.reshape(depth, tile, width)
        store(j).start()

    for j in range(CHUNKS):
        project(j)
        if j >= 1:
            finish_x(j - 1)
            if j == 1:
                seam.start()
        if j >= 2:
            finish_y(j - 2)
    finish_x(CHUNKS - 1)
    finish_y(CHUNKS - 2)
    finish_y(CHUNKS - 1)
    for j in range(CHUNKS):
        both(functools.partial(image_copy, j), "send", None)
        both(functools.partial(halo_copy, j), "send", None)
        store(j).wait()
    seam.wait_send()


def per_device(n_gx, images, weights, crossings, counts):
    cams, tile, cols = images.shape
    depth, slots, sub = weights.shape[1:4]
    width, blocks = cols // CHUNKS, tile // sub + 2
    rows = depth * tile
    anywhere = pl.BlockSpec(memory_space=pl.ANY)
    scalars = pl.BlockSpec(memory_space=pltpu.SMEM)
    return pl.pallas_call(
        functools.partial(kernel, (cams, depth, slots, sub, tile, cols, n_gx)),
        out_shape=jax.ShapeDtypeStruct((depth, tile, cols), F32),
        in_specs=[scalars, scalars, anywhere, anywhere],
        out_specs=anywhere,
        scratch_shapes=[
            pltpu.VMEM((cams, blocks * sub, cols), BF),
            pltpu.VMEM(weights.shape, BF),
            pltpu.VMEM((cams, rows, blocks * sub), BF),
            pltpu.VMEM((rows, width), F32),
            pltpu.VMEM((2, rows, width), BF),
            pltpu.VMEM((2, rows, cols + 2 * LANES), BF),
            pltpu.VMEM((2, rows, width), F32),
            pltpu.VMEM((CHUNKS, depth, tile, width), F32),
            pltpu.VMEM((width + 2 * LANES, width), BF),
            pltpu.VMEM((tile, tile), BF),
            pltpu.VMEM((width + 2 * LANES, width), BF),
            pltpu.VMEM((32, rows), BF),
            pltpu.VMEM((rows, 32), BF),
            pltpu.VMEM((CHUNKS, 32, width), BF),
            pltpu.VMEM((CHUNKS, 32, width), BF),
            pltpu.SemaphoreType.DMA((2, CHUNKS)),
            pltpu.SemaphoreType.DMA((2, CHUNKS)),
            pltpu.SemaphoreType.DMA((2, CHUNKS)),
            pltpu.SemaphoreType.DMA((2, CHUNKS)),
            pltpu.SemaphoreType.DMA((2,)),
            pltpu.SemaphoreType.DMA((2,)),
            pltpu.SemaphoreType.DMA((CHUNKS,)),
        ],
        compiler_params=pltpu.CompilerParams(
            collective_id=0, has_side_effects=True, vmem_limit_bytes=60 * 2**20
        ),
    )(
        jnp.transpose(crossings, (0, 3, 2, 1)),
        jnp.transpose(counts, (0, 2, 1)),
        images,
        weights,
    )


def solution(mesh):
    in_specs = (
        P("grp", "gx", "gy"),
        P(None, None, None, None, "gx"),
        P(None, None, "gx", None),
        P(None, None, "gx"),
    )
    return jax.shard_map(
        functools.partial(per_device, mesh.shape["gx"]),
        mesh=mesh, in_specs=in_specs, out_specs=P("grp", "gx", "gy"), check_vma=False
    )
```

```python
import functools

import jax
import jax.numpy as jnp
import numpy as np
from jax import lax
from jax.experimental import pallas as pl
from jax.experimental.pallas import tpu as pltpu
from jax.sharding import PartitionSpec as P

PASSES = 3
CHUNKS = 4
LANES = 128
BF = jnp.bfloat16
F32 = jnp.float32


def taps(distance):
    distance = jnp.abs(distance)
    value = jnp.where(distance == 0, 20.0, 0.0)
    for far, weight in ((1, 15.0), (2, 6.0), (3, 1.0)):
        value = jnp.where(distance == far, weight, value)
    return value.astype(F32)


def iota(shape, dim):
    return lax.broadcasted_iota(jnp.int32, shape, dim)


def layer_matrix(depth):
    step = 0.5 * np.eye(depth) + 0.25 * (np.eye(depth, k=1) + np.eye(depth, k=-1))
    return np.linalg.matrix_power(step, PASSES)


def split(value):
    high = value.astype(BF)
    return high, (value - high.astype(F32)).astype(BF)


def dot(a, b):
    return jnp.dot(a, b, preferred_element_type=F32)


def kernel(dims, lists, counts, images, weights, out,
           window, stack, spread, prod, part, field, done, out_stage, across, along, edge, pick, beside,
           outbox, inbox, img_send, img_recv, halo_send, halo_recv, seam_sem, local_sem, out_sem):
    cams, depth, slots, sub, tile, cols, n_gx = dims
    width = cols // CHUNKS
    blocks = tile // sub + 2
    gx, gy = lax.axis_index("gx"), lax.axis_index("gy")
    has_lo, has_hi = gx > 0, gx < n_gx - 1
    first = jnp.where(has_lo, 0.0, 1.0).astype(F32)
    last = jnp.where(has_hi, 0.0, 1.0).astype(F32)
    lo, hi, peer = {"gx": gx - 1}, {"gx": gx + 1}, {"gy": 1 - gy}

    def offset(j):
        return pl.multiple_of(jnp.where(gy == 0, (CHUNKS - 1 - j) * width, j * width), width)

    barrier = pltpu.get_barrier_semaphore()

    @pl.when(has_lo)
    def _():
        pl.semaphore_signal(barrier, inc=1, device_id=lo, device_id_type=pl.DeviceIdType.MESH)

    @pl.when(has_hi)
    def _():
        pl.semaphore_signal(barrier, inc=1, device_id=hi, device_id_type=pl.DeviceIdType.MESH)

    pl.semaphore_signal(barrier, inc=1, device_id=peer, device_id_type=pl.DeviceIdType.MESH)

    load_w = pltpu.make_async_copy(weights, stack, local_sem.at[0])
    load_i = pltpu.make_async_copy(images, window.at[:, pl.ds(sub, tile), :], local_sem.at[1])
    load_w.start()
    load_i.start()

    pl.semaphore_wait(barrier, 1 + jnp.where(has_lo, 1, 0) + jnp.where(has_hi, 1, 0))

    def remote(src, dst, send, recv, where):
        return pltpu.make_async_remote_copy(
            src_ref=src, dst_ref=dst, send_sem=send, recv_sem=recv,
            device_id=where, device_id_type=pl.DeviceIdType.MESH)

    def image_copy(j, up):
        cut = pl.ds(offset(j), width)
        if up:
            return remote(images.at[:, pl.ds(tile - sub, sub), cut], window.at[:, pl.ds(0, sub), cut],
                          img_send.at[0, j], img_recv.at[0, j], hi)
        return remote(images.at[:, pl.ds(0, sub), cut], window.at[:, pl.ds(tile + sub, sub), cut],
                      img_send.at[1, j], img_recv.at[1, j], lo)

    def halo_copy(j, up):
        if up:
            return remote(outbox.at[j, pl.ds(16, 16)], inbox.at[j, pl.ds(0, 16)],
                          halo_send.at[0, j], halo_recv.at[0, j], hi)
        return remote(outbox.at[j, pl.ds(0, 16)], inbox.at[j, pl.ds(16, 16)],
                      halo_send.at[1, j], halo_recv.at[1, j], lo)

    def both(make, send, recv):
        def act(copy, start, finish):
            if start:
                copy.start()
            if finish == "send":
                copy.wait_send()
            if finish == "recv":
                copy.wait_recv()

        if send is not None:
            pl.when(has_hi)(lambda: act(make(True), send == "start", send))
            pl.when(has_lo)(lambda: act(make(False), send == "start", send))
        if recv is not None:
            pl.when(has_lo)(lambda: act(make(True), False, "recv"))
            pl.when(has_hi)(lambda: act(make(False), False, "recv"))

    for j in range(CHUNKS):
        both(functools.partial(image_copy, j), "start", None)

    @pl.when(jnp.logical_not(has_lo))
    def _():
        window[:, pl.ds(0, sub), :] = jnp.zeros((cams, sub, cols), BF)
        inbox[:, pl.ds(0, 16), :] = jnp.zeros((CHUNKS, 16, width), BF)

    @pl.when(jnp.logical_not(has_hi))
    def _():
        window[:, pl.ds(tile + sub, sub), :] = jnp.zeros((cams, sub, cols), BF)
        inbox[:, pl.ds(16, 16), :] = jnp.zeros((CHUNKS, 16, width), BF)

    outer = pl.multiple_of(jnp.where(gy == 0, 0, cols + LANES), LANES)
    inner = pl.multiple_of(jnp.where(gy == 0, cols + LANES, 0), LANES)
    field[:, :, pl.ds(outer, LANES)] = jnp.zeros((2, depth * tile, LANES), BF)

    i, k = iota((tile, tile), 0), iota((tile, tile), 1)
    along[...] = ((taps(i - k) - first * taps(i + k + 2) - last * taps(2 * tile - i - k)) / 64).astype(BF)
    r, k = iota((depth * tile, 32), 0), iota((depth * tile, 32), 1)
    q, zz = k % 4, (k // 4) % depth
    place = jnp.where(k < 16, q - 3, tile + q)
    near = jnp.where((q < 3) & (zz == r // tile), taps(r % tile - place), 0.0)
    beside[...] = (near / 64).astype(BF)
    k, r = iota((32, depth * tile), 0), iota((32, depth * tile), 1)
    q, zz = k % 4, (k // 4) % depth
    place = zz * tile + jnp.where(k < 16, q, tile - 3 + q)
    pick[...] = jnp.where((q < 3) & (place == r), 1.0, 0.0).astype(BF)
    a, b = iota((width + 2 * LANES, width), 0) - LANES, iota((width + 2 * LANES, width), 1)
    across[...] = (taps(a - b) / 64).astype(BF)
    mirror = jnp.where(gy == 0, a + b + 2, 2 * width - a - b)
    mirror = jnp.where((a >= 0) & (a < width), mirror, 4)
    edge[...] = ((taps(a - b) - taps(mirror)) / 64).astype(BF)

    load_w.wait()
    for c in range(cams):
        for z in range(depth):
            mats = [stack[c, z, s].astype(F32) for s in range(slots)]
            rows = []
            for w in range(blocks):
                total = None
                for s in range(slots):
                    used = (lists[c, s, 0, z] == w) & (s < counts[c, 0, z])
                    term = mats[s] * jnp.where(used, 1.0, 0.0).astype(F32)
                    total = term if total is None else total + term
                rows.append(total)
            whole = jnp.concatenate(rows, axis=0)
            spread[c, pl.ds(z * tile, tile), :] = jnp.transpose(whole).astype(BF)
    load_i.wait()

    layers = layer_matrix(depth)

    def project(j):
        cut = pl.ds(offset(j), width)
        both(functools.partial(image_copy, j), None, "recv")
        for c in range(cams):
            now = dot(spread[c], window[c, :, cut])
            if c == 0:
                prod[...] = now
            else:
                prod[...] = prod[...] * now
        for z in range(depth):
            total = None
            for s in range(depth):
                if layers[z, s] != 0.0:
                    term = prod[pl.ds(s * tile, tile), :] * float(layers[z, s])
                    total = term if total is None else total + term
            high, low = split(total)
            part[0, pl.ds(z * tile, tile), :] = high
            part[1, pl.ds(z * tile, tile), :] = low
        outbox[j] = dot(pick[...], part[0]).astype(BF)
        both(functools.partial(halo_copy, j), "start", None)
        for z in range(depth):
            rows = pl.ds(z * tile, tile)
            done[j, rows, :] = dot(along[...], part[0, rows, :]) + dot(along[...], part[1, rows, :])

    def finish_x(j):
        both(functools.partial(halo_copy, j), None, "recv")
        high, low = split(done[j] + dot(beside[...], inbox[j]))
        cut = pl.ds(pl.multiple_of(offset(j) + LANES, LANES), width)
        field[0, :, cut] = high
        field[1, :, cut] = low

    mine = pl.multiple_of(jnp.where(gy == 0, cols, LANES), LANES)
    theirs = pl.multiple_of(jnp.where(gy == 0, 0, cols + LANES), LANES)
    seam = remote(field.at[:, :, pl.ds(mine, LANES)], field.at[:, :, pl.ds(theirs, LANES)],
                  seam_sem.at[0], seam_sem.at[1], peer)

    def store(j):
        return pltpu.make_async_copy(
            out_stage.at[j], out.at[:, :, pl.ds(offset(j), width)], out_sem.at[j])

    def finish_y(j):
        if j == 0:
            seam.wait_recv()
        cut = pl.ds(offset(j), width + 2 * LANES)
        mat = (edge if j == CHUNKS - 1 else across)[...]
        full = dot(field[0, :, cut], mat) + dot(field[1, :, cut], mat)
        out_stage[j] = full.reshape(depth, tile, width)
        store(j).start()

    for j in range(CHUNKS):
        project(j)
    for j in range(CHUNKS):
        finish_x(j)
        if j == 0:
            seam.start()
        if j >= 1:
            finish_y(j - 1)
    finish_y(CHUNKS - 1)
    for j in range(CHUNKS):
        both(functools.partial(image_copy, j), "send", None)
        both(functools.partial(halo_copy, j), "send", None)
        store(j).wait()
    seam.wait_send()


def per_device(n_gx, images, weights, crossings, counts):
    cams, tile, cols = images.shape
    depth, slots, sub = weights.shape[1:4]
    width, blocks = cols // CHUNKS, tile // sub + 2
    rows = depth * tile
    anywhere = pl.BlockSpec(memory_space=pl.ANY)
    scalars = pl.BlockSpec(memory_space=pltpu.SMEM)
    return pl.pallas_call(
        functools.partial(kernel, (cams, depth, slots, sub, tile, cols, n_gx)),
        out_shape=jax.ShapeDtypeStruct((depth, tile, cols), F32),
        in_specs=[scalars, scalars, anywhere, anywhere],
        out_specs=anywhere,
        scratch_shapes=[
            pltpu.VMEM((cams, blocks * sub, cols), BF),
            pltpu.VMEM(weights.shape, BF),
            pltpu.VMEM((cams, rows, blocks * sub), BF),
            pltpu.VMEM((rows, width), F32),
            pltpu.VMEM((2, rows, width), BF),
            pltpu.VMEM((2, rows, cols + 2 * LANES), BF),
            pltpu.VMEM((CHUNKS, rows, width), F32),
            pltpu.VMEM((CHUNKS, depth, tile, width), F32),
            pltpu.VMEM((width + 2 * LANES, width), BF),
            pltpu.VMEM((tile, tile), BF),
            pltpu.VMEM((width + 2 * LANES, width), BF),
            pltpu.VMEM((32, rows), BF),
            pltpu.VMEM((rows, 32), BF),
            pltpu.VMEM((CHUNKS, 32, width), BF),
            pltpu.VMEM((CHUNKS, 32, width), BF),
            pltpu.SemaphoreType.DMA((2, CHUNKS)),
            pltpu.SemaphoreType.DMA((2, CHUNKS)),
            pltpu.SemaphoreType.DMA((2, CHUNKS)),
            pltpu.SemaphoreType.DMA((2, CHUNKS)),
            pltpu.SemaphoreType.DMA((2,)),
            pltpu.SemaphoreType.DMA((2,)),
            pltpu.SemaphoreType.DMA((CHUNKS,)),
        ],
        compiler_params=pltpu.CompilerParams(
            collective_id=0, has_side_effects=True, vmem_limit_bytes=60 * 2**20
        ),
    )(
        jnp.transpose(crossings, (0, 3, 2, 1)),
        jnp.transpose(counts, (0, 2, 1)),
        images,
        weights,
    )


def solution(mesh):
    in_specs = (
        P("grp", "gx", "gy"),
        P(None, None, None, None, "gx"),
        P(None, None, "gx", None),
        P(None, None, "gx"),
    )
    return jax.shard_map(
        functools.partial(per_device, mesh.shape["gx"]),
        mesh=mesh, in_specs=in_specs, out_specs=P("grp", "gx", "gy"), check_vma=False
    )
```

```python
import functools

import jax
import jax.numpy as jnp
import numpy as np
from jax import lax
from jax.experimental import pallas as pl
from jax.experimental.pallas import tpu as pltpu
from jax.sharding import PartitionSpec as P

PASSES = 3
CHUNKS = 4
LANES = 128
BF = jnp.bfloat16
F32 = jnp.float32


def taps(distance):
    distance = jnp.abs(distance)
    value = jnp.where(distance == 0, 20.0, 0.0)
    for far, weight in ((1, 15.0), (2, 6.0), (3, 1.0)):
        value = jnp.where(distance == far, weight, value)
    return value.astype(F32)


def iota(shape, dim):
    return lax.broadcasted_iota(jnp.int32, shape, dim)


def layer_matrix(depth):
    step = 0.5 * np.eye(depth) + 0.25 * (np.eye(depth, k=1) + np.eye(depth, k=-1))
    return np.linalg.matrix_power(step, PASSES)


def split(value):
    high = value.astype(BF)
    return high, (value - high.astype(F32)).astype(BF)


def dot(a, b):
    return jnp.dot(a, b, preferred_element_type=F32)


def kernel(dims, lists, counts, images, weights, out,
           window, stack, spread, prod, part, field, done, out_stage, across, along, edge, pick, beside,
           outbox, inbox, img_send, img_recv, halo_send, halo_recv, seam_sem, local_sem, out_sem):
    cams, depth, slots, sub, tile, cols, n_gx = dims
    width = cols // CHUNKS
    blocks = tile // sub + 2
    gx, gy = lax.axis_index("gx"), lax.axis_index("gy")
    has_lo, has_hi = gx > 0, gx < n_gx - 1
    first = jnp.where(has_lo, 0.0, 1.0).astype(F32)
    last = jnp.where(has_hi, 0.0, 1.0).astype(F32)
    lo, hi, peer = {"gx": gx - 1}, {"gx": gx + 1}, {"gy": 1 - gy}

    def offset(j):
        return pl.multiple_of(jnp.where(gy == 0, (CHUNKS - 1 - j) * width, j * width), width)

    barrier = pltpu.get_barrier_semaphore()

    @pl.when(has_lo)
    def _():
        pl.semaphore_signal(barrier, inc=1, device_id=lo, device_id_type=pl.DeviceIdType.MESH)

    @pl.when(has_hi)
    def _():
        pl.semaphore_signal(barrier, inc=1, device_id=hi, device_id_type=pl.DeviceIdType.MESH)

    pl.semaphore_signal(barrier, inc=1, device_id=peer, device_id_type=pl.DeviceIdType.MESH)

    load_w = pltpu.make_async_copy(weights, stack, local_sem.at[0])
    load_i = pltpu.make_async_copy(images, window.at[:, pl.ds(sub, tile), :], local_sem.at[1])
    load_w.start()
    load_i.start()

    pl.semaphore_wait(barrier, 1 + jnp.where(has_lo, 1, 0) + jnp.where(has_hi, 1, 0))

    def remote(src, dst, send, recv, where):
        return pltpu.make_async_remote_copy(
            src_ref=src, dst_ref=dst, send_sem=send, recv_sem=recv,
            device_id=where, device_id_type=pl.DeviceIdType.MESH)

    def image_copy(j, up):
        cut = pl.ds(offset(j), width)
        if up:
            return remote(images.at[:, pl.ds(tile - sub, sub), cut], window.at[:, pl.ds(0, sub), cut],
                          img_send.at[0, j], img_recv.at[0, j], hi)
        return remote(images.at[:, pl.ds(0, sub), cut], window.at[:, pl.ds(tile + sub, sub), cut],
                      img_send.at[1, j], img_recv.at[1, j], lo)

    def halo_copy(j, up):
        if up:
            return remote(outbox.at[j, pl.ds(16, 16)], inbox.at[j, pl.ds(0, 16)],
                          halo_send.at[0, j], halo_recv.at[0, j], hi)
        return remote(outbox.at[j, pl.ds(0, 16)], inbox.at[j, pl.ds(16, 16)],
                      halo_send.at[1, j], halo_recv.at[1, j], lo)

    def both(make, send, recv):
        def act(copy, start, finish):
            if start:
                copy.start()
            if finish == "send":
                copy.wait_send()
            if finish == "recv":
                copy.wait_recv()

        if send is not None:
            pl.when(has_hi)(lambda: act(make(True), send == "start", send))
            pl.when(has_lo)(lambda: act(make(False), send == "start", send))
        if recv is not None:
            pl.when(has_lo)(lambda: act(make(True), False, "recv"))
            pl.when(has_hi)(lambda: act(make(False), False, "recv"))

    for j in range(CHUNKS):
        both(functools.partial(image_copy, j), "start", None)

    @pl.when(jnp.logical_not(has_lo))
    def _():
        window[:, pl.ds(0, sub), :] = jnp.zeros((cams, sub, cols), BF)
        inbox[:, pl.ds(0, 16), :] = jnp.zeros((CHUNKS, 16, width), BF)

    @pl.when(jnp.logical_not(has_hi))
    def _():
        window[:, pl.ds(tile + sub, sub), :] = jnp.zeros((cams, sub, cols), BF)
        inbox[:, pl.ds(16, 16), :] = jnp.zeros((CHUNKS, 16, width), BF)

    outer = pl.multiple_of(jnp.where(gy == 0, 0, cols + LANES), LANES)
    inner = pl.multiple_of(jnp.where(gy == 0, cols + LANES, 0), LANES)
    field[:, :, pl.ds(outer, LANES)] = jnp.zeros((2, depth * tile, LANES), BF)

    i, k = iota((tile, tile), 0), iota((tile, tile), 1)
    along[...] = ((taps(i - k) - first * taps(i + k + 2) - last * taps(2 * tile - i - k)) / 64).astype(BF)
    r, k = iota((depth * tile, 32), 0), iota((depth * tile, 32), 1)
    q, zz = k % 4, (k // 4) % depth
    place = jnp.where(k < 16, q - 3, tile + q)
    near = jnp.where((q < 3) & (zz == r // tile), taps(r % tile - place), 0.0)
    beside[...] = (near / 64).astype(BF)
    k, r = iota((32, depth * tile), 0), iota((32, depth * tile), 1)
    q, zz = k % 4, (k // 4) % depth
    place = zz * tile + jnp.where(k < 16, q, tile - 3 + q)
    pick[...] = jnp.where((q < 3) & (place == r), 1.0, 0.0).astype(BF)
    a, b = iota((width + 2 * LANES, width), 0) - LANES, iota((width + 2 * LANES, width), 1)
    across[...] = (taps(a - b) / 64).astype(BF)
    mirror = jnp.where(gy == 0, a + b + 2, 2 * width - a - b)
    mirror = jnp.where((a >= 0) & (a < width), mirror, 4)
    edge[...] = ((taps(a - b) - taps(mirror)) / 64).astype(BF)

    load_w.wait()
    for c in range(cams):
        for z in range(depth):
            mats = [stack[c, z, s].astype(F32) for s in range(slots)]
            rows = []
            for w in range(blocks):
                total = None
                for s in range(slots):
                    used = (lists[c, s, 0, z] == w) & (s < counts[c, 0, z])
                    term = mats[s] * jnp.where(used, 1.0, 0.0).astype(F32)
                    total = term if total is None else total + term
                rows.append(total)
            whole = jnp.concatenate(rows, axis=0)
            spread[c, pl.ds(z * tile, tile), :] = jnp.transpose(whole).astype(BF)
    load_i.wait()

    layers = layer_matrix(depth)

    def put(j, rows, value):
        high, low = split(value)
        cut = pl.ds(pl.multiple_of(offset(j) + LANES, LANES), width)
        field[0, rows, cut] = high
        field[1, rows, cut] = low

    def project(j):
        cut = pl.ds(offset(j), width)
        both(functools.partial(image_copy, j), None, "recv")
        for c in range(cams):
            now = dot(spread[c], window[c, :, cut])
            if c == 0:
                prod[...] = now
            else:
                prod[...] = prod[...] * now
        for z in range(depth):
            total = None
            for s in range(depth):
                if layers[z, s] != 0.0:
                    term = prod[pl.ds(s * tile, tile), :] * float(layers[z, s])
                    total = term if total is None else total + term
            high, low = split(total)
            part[0, pl.ds(z * tile, tile), :] = high
            part[1, pl.ds(z * tile, tile), :] = low
        outbox[j] = dot(pick[...], part[0]).astype(BF)
        both(functools.partial(halo_copy, j), "start", None)
        for z in range(depth):
            rows = pl.ds(z * tile, tile)
            done[j, rows, :] = dot(along[...], part[0, rows, :]) + dot(along[...], part[1, rows, :])
        put(j, pl.ds(0, depth * tile), done[j])

    def finish_x(j):
        both(functools.partial(halo_copy, j), None, "recv")
        for z in range(depth):
            for start in (0, tile - 16):
                rows = pl.ds(z * tile + start, 16)
                put(j, rows, done[j, rows, :] + dot(beside[rows, :], inbox[j]))

    mine = pl.multiple_of(jnp.where(gy == 0, cols, LANES), LANES)
    theirs = pl.multiple_of(jnp.where(gy == 0, 0, cols + LANES), LANES)
    seam = remote(field.at[:, :, pl.ds(mine, LANES)], field.at[:, :, pl.ds(theirs, LANES)],
                  seam_sem.at[0], seam_sem.at[1], peer)

    def store(j):
        return pltpu.make_async_copy(
            out_stage.at[j], out.at[:, :, pl.ds(offset(j), width)], out_sem.at[j])

    def finish_y(j):
        if j == 0:
            seam.wait_recv()
        cut = pl.ds(offset(j), width + 2 * LANES)
        mat = (edge if j == CHUNKS - 1 else across)[...]
        full = dot(field[0, :, cut], mat) + dot(field[1, :, cut], mat)
        out_stage[j] = full.reshape(depth, tile, width)
        store(j).start()

    for j in range(CHUNKS):
        project(j)
    for j in range(CHUNKS):
        finish_x(j)
        if j == 0:
            seam.start()
        if j >= 1:
            finish_y(j - 1)
    finish_y(CHUNKS - 1)
    for j in range(CHUNKS):
        both(functools.partial(image_copy, j), "send", None)
        both(functools.partial(halo_copy, j), "send", None)
        store(j).wait()
    seam.wait_send()


def per_device(n_gx, images, weights, crossings, counts):
    cams, tile, cols = images.shape
    depth, slots, sub = weights.shape[1:4]
    width, blocks = cols // CHUNKS, tile // sub + 2
    rows = depth * tile
    anywhere = pl.BlockSpec(memory_space=pl.ANY)
    scalars = pl.BlockSpec(memory_space=pltpu.SMEM)
    return pl.pallas_call(
        functools.partial(kernel, (cams, depth, slots, sub, tile, cols, n_gx)),
        out_shape=jax.ShapeDtypeStruct((depth, tile, cols), F32),
        in_specs=[scalars, scalars, anywhere, anywhere],
        out_specs=anywhere,
        scratch_shapes=[
            pltpu.VMEM((cams, blocks * sub, cols), BF),
            pltpu.VMEM(weights.shape, BF),
            pltpu.VMEM((cams, rows, blocks * sub), BF),
            pltpu.VMEM((rows, width), F32),
            pltpu.VMEM((2, rows, width), BF),
            pltpu.VMEM((2, rows, cols + 2 * LANES), BF),
            pltpu.VMEM((CHUNKS, rows, width), F32),
            pltpu.VMEM((CHUNKS, depth, tile, width), F32),
            pltpu.VMEM((width + 2 * LANES, width), BF),
            pltpu.VMEM((tile, tile), BF),
            pltpu.VMEM((width + 2 * LANES, width), BF),
            pltpu.VMEM((32, rows), BF),
            pltpu.VMEM((rows, 32), BF),
            pltpu.VMEM((CHUNKS, 32, width), BF),
            pltpu.VMEM((CHUNKS, 32, width), BF),
            pltpu.SemaphoreType.DMA((2, CHUNKS)),
            pltpu.SemaphoreType.DMA((2, CHUNKS)),
            pltpu.SemaphoreType.DMA((2, CHUNKS)),
            pltpu.SemaphoreType.DMA((2, CHUNKS)),
            pltpu.SemaphoreType.DMA((2,)),
            pltpu.SemaphoreType.DMA((2,)),
            pltpu.SemaphoreType.DMA((CHUNKS,)),
        ],
        compiler_params=pltpu.CompilerParams(
            collective_id=0, has_side_effects=True, vmem_limit_bytes=60 * 2**20
        ),
    )(
        jnp.transpose(crossings, (0, 3, 2, 1)),
        jnp.transpose(counts, (0, 2, 1)),
        images,
        weights,
    )


def solution(mesh):
    in_specs = (
        P("grp", "gx", "gy"),
        P(None, None, None, None, "gx"),
        P(None, None, "gx", None),
        P(None, None, "gx"),
    )
    return jax.shard_map(
        functools.partial(per_device, mesh.shape["gx"]),
        mesh=mesh, in_specs=in_specs, out_specs=P("grp", "gx", "gy"), check_vma=False
    )
```
